512 devices in a mesh: frame: 128 (over x, y_hi, z), head: 4 (over y_lo, core).
Axes of the slice: x: 4, y: 8 (y_hi: 4, y_lo: 2; y = y_hi * 2 + y_lo), z: 8, core: 2. Of those that a mesh axis runs over, the one named last changes fastest.
Arguments:
- encoded: bfloat16 [262144, 1152], P(('frame', 'head')), may hold values from -32 to 32
- block_source: int32 [512, 1], P('frame'), may hold values from 0 to 3; in each aligned block of 4 rows (0 to 3, 4 to 7, ...) at most 2 rows name the same one
- block_slot: int32 [128, 4, 4], P('frame'), may hold values from 0 to 3, each once within a row
- video_patches: int32 [3], replicated, may hold values from 1 to 32768, 65536 in all
- latent_video: int32 [384], replicated, may hold values from 0 to 2, as said below
- media_gain: float32 [1152], replicated, may hold values from 0.5 to 1.5
- queries: bfloat16 [768, 4096], P('frame', 'head'), may hold values from -160 to 160
- w_key: bfloat16 [1152, 4096], P('frame', 'head'), may hold values from -0.1875 to 0.1875
- w_value: bfloat16 [1152, 4096], P('frame', 'head'), may hold values from -0.1875 to 0.1875
Outputs:
- attended: bfloat16 [768, 4096], P('frame', 'head')
The draws below stay inside these ranges and needn't reach their ends.
Inputs may be any that keep to these rules, and one draw needn't show every extreme that they name: `block_source`: within the 4 blocks of one frame shard no source is named more than 2 times. Each row block_slot[f, s, :] holds every offset once. `video_patches`: the counts sum to 65536. `latent_video`: every video owns exactly 256 latents.
All inputs are finite; a program needn't handle non-finite values.
Results may differ from the reference program's by a relative error of at most 0.011.
Values may be sent and summed in bfloat16 or wider, within the bound.
No kernel may reach another device: no remote copies, remote signals or barrier semaphores. Data moves between devices by JAX's collectives and lax.ppermute only.
A program may use at most 64 MiB of HBM per device.

```python
import math
import jax
import jax.numpy as jnp
import numpy as np
from jax import lax

D = 4096
HEADS = 32
HEAD_DIM = 128
MEDIA = 1152
NUM_LAT = 256
VIDEOS = 3
LAT_BLK = 2
BLK_ROWS = 128
NB = 4
CAP = 2
PATCHES = 65536
LAT = 768
LAT_BLKS = 384
PATCH_BLKS = 512
ENC_ALL = 262144
N_FRAME = 128
N_HEAD = 4


def draw_encoded(key, part):
    key = jax.random.fold_in(key, 11)
    first = jax.random.fold_in(key, 0)
    values = jnp.clip(jax.random.normal(first, (ENC_ALL, MEDIA), jnp.float32), -8.0, 8.0)
    return values.astype(jnp.bfloat16)


def draw_latent_video(key, part):
    key = jax.random.fold_in(key, 37)
    order = jax.random.permutation(key, LAT_BLKS)
    return (order // (NUM_LAT // LAT_BLK)).astype(jnp.int32)


def draw_queries(key, part):
    key = jax.random.fold_in(key, 23)
    first = jax.random.fold_in(key, 0)
    values = jnp.clip(1.5 * jax.random.normal(first, (LAT, D), jnp.float32), -12.0, 12.0)
    return values.astype(jnp.bfloat16)


def block_scale(own_key, extent, cuts, least, top_value):
    gain = 1.0
    for dim, shards_of in cuts:
        steps = jax.random.uniform(jax.random.fold_in(jax.random.fold_in(own_key, 6), dim), (shards_of,), jnp.float32, least / len(cuts), top_value / len(cuts))
        gain = gain * jnp.repeat(jnp.exp(steps), extent[dim] // shards_of).reshape((-1,) + (1,) * (len(extent) - 1 - dim))
    return gain


def length_profile(count, total, reach, skew):
    portions = [(1 << 20) // math.isqrt(grade ** skew) + 1 for grade in range(2, count + 1)]
    rest, counts = total - reach - (count - 1), [1] * (count - 1)
    while rest > 0:
        movable = [i for i in range(count - 1) if counts[i] < reach]
        mass, budget = sum([portions[i] for i in movable]), rest
        for i in movable:
            extra = min(reach - counts[i], max(1, budget * portions[i] // mass), rest)
            counts[i] = counts[i] + extra
            rest = rest - extra
    return np.array([reach] + counts)


def ragged(rng, amount, total, limit, slope):
    if amount == 2:
        one = jax.random.randint(rng, (), max(1, total - limit), min(limit, total - 1) + 1)
        return jnp.stack([one, total - one])
    tallies = jnp.asarray(length_profile(amount, total, limit, slope), jnp.int32)
    twos = (amount - 1) // 2
    giver, sink = tallies[1:1 + 2 * twos:2], tallies[2:2 + 2 * twos:2]
    margin = jnp.minimum(giver - 1, limit - sink)
    passed = jax.random.randint(jax.random.fold_in(rng, 1), (twos,), 0, 1 << 20) % (margin + 1)
    tallies = tallies.at[1:1 + 2 * twos:2].set(giver - passed).at[2:2 + 2 * twos:2].set(sink + passed)
    return tallies[jax.random.permutation(jax.random.fold_in(rng, 2), amount)]


def assign_block(key, own, number, rows, amount, top, limit, skew):
    order = jax.random.permutation(key, amount)
    packed, usual = portions_of(amount, rows * top, limit, skew, True), portions_of(amount, rows * top, limit, skew, False)
    places = jnp.arange(amount)

    def named(lengths, offset_by):
        used = int((lengths > 0).sum())
        fixed = max(1, used // 4)
        moved = fixed + (places - fixed + offset_by * (used - fixed)) % max(1, amount - fixed)
        return jnp.zeros((amount,), jnp.int32).at[order[jnp.where(places < fixed, places, moved)]].set(jnp.asarray(lengths, jnp.int32))

    lengths = jnp.where(number % 4 == 0, named(packed, number // 4), named(usual, number - number // 4 - 1))
    mixed = jax.random.permutation(jax.random.fold_in(own, 3), amount)
    source_of, taker = mixed[0:amount // 2 * 2:2], mixed[1:amount // 2 * 2:2]
    margin = jnp.minimum(lengths[source_of] - 1, limit - lengths[taker]) // 2
    margin = jnp.where((source_of == order[0]) | (taker == order[0]) | (lengths[taker] == 0), 0, jnp.maximum(margin, 0))
    moved = jax.random.randint(jax.random.fold_in(own, 4), (amount // 2,), 0, 1 << 20) % (margin + 1)
    lengths = lengths.at[source_of].add(-moved).at[taker].add(moved)
    members = jnp.searchsorted(jnp.cumsum(lengths), jnp.arange(rows * top), side="right").astype(jnp.int32)
    grid = members.reshape(top, rows).T
    grid = grid[jax.random.permutation(jax.random.fold_in(own, 1), rows)]
    offset_by = jax.random.randint(jax.random.fold_in(own, 2), (rows, 1), 0, top)
    return jnp.take_along_axis(grid, (jnp.arange(top)[None, :] + offset_by) % top, axis=1)


def portions_of(number_of, total, bound, skew, full):
    loads = [(1 << 20) // math.isqrt(grade ** skew) + 1 for grade in range(1, number_of + 1)]
    largest = bound if full else min(bound, max(-(-total // number_of), total * loads[0] // sum(loads)))
    least = 1 if total - largest >= number_of - 1 else 0
    counts, spare = [largest] + [least] * (number_of - 1), total - largest - least * (number_of - 1)
    while spare > 0:
        candidates = [i for i in range(1, number_of) if counts[i] < largest] or [i for i in range(1, number_of) if counts[i] < bound]
        whole, left = sum([loads[i] for i in candidates]), spare
        for i in candidates:
            addition = min(bound - counts[i], max(1, left * loads[i] // whole), spare)
            counts[i] = counts[i] + addition
            spare = spare - addition
    return np.array(counts)


def noise(own_key, dims, deviation, reach, cuts=(), kind=jnp.bfloat16):
    level = block_scale(own_key, dims, cuts, -0.22, 0.18) if cuts else 1.0
    array = jax.random.normal(own_key, dims, jnp.float32) * deviation * level
    return jnp.minimum(jnp.maximum(array, -reach), reach).astype(kind)


def setup_inputs(seed: int = 0) -> dict:
    key_of = jax.random.split(jax.random.key(seed), 10)
    encoded = draw_encoded(jax.random.fold_in(key_of[9], 71), 0)
    block_source_keys = jax.random.split(jax.random.fold_in(key_of[1], 1), PATCH_BLKS // NB)
    block_source_turns = jax.random.permutation(jax.random.fold_in(key_of[1], 3), PATCH_BLKS // NB)
    block_source = jax.vmap(lambda own, number: assign_block(jax.random.fold_in(key_of[1], 2), own, number, NB, N_HEAD, 1, CAP, 2))(block_source_keys, block_source_turns).reshape((PATCH_BLKS, 1))
    block_slot = jax.vmap(lambda own: jax.random.permutation(own, NB))(jax.random.split(key_of[2], N_FRAME * N_HEAD)).reshape((N_FRAME, N_HEAD, NB)).astype(jnp.int32)
    video_patches = ragged(key_of[3], VIDEOS, PATCHES, PATCHES // 2, 2).astype(jnp.int32)
    latent_video = draw_latent_video(jax.random.fold_in(key_of[9], 71), 0)
    media_gain = jnp.clip(1.0 + 0.1 * jax.random.normal(key_of[5], (MEDIA,), jnp.float32), 0.5, 1.5)
    queries = draw_queries(jax.random.fold_in(key_of[9], 71), 0)
    w_key = noise(key_of[7], (MEDIA, D), MEDIA ** -0.5, 0.1875, ((0, 128), (1, 4)))
    w_value = noise(key_of[8], (MEDIA, D), MEDIA ** -0.5, 0.1875, ((0, 128), (1, 4)))
    return dict(encoded=encoded, block_source=block_source, block_slot=block_slot, video_patches=video_patches, latent_video=latent_video, media_gain=media_gain, queries=queries, w_key=w_key, w_value=w_value)


def layer_norm(rows, media_gain):
    values = rows.astype(jnp.float32)
    center = values - lax.optimization_barrier(jnp.mean(values, axis=1, keepdims=True))
    spread = lax.optimization_barrier(jnp.mean(center * center, axis=1, keepdims=True))
    return (center * lax.rsqrt(spread + 1e-06) * media_gain.astype(jnp.float32)).astype(jnp.bfloat16)

def reference(encoded, block_source, block_slot, video_patches, latent_video, media_gain, queries, w_key, w_value):
    source = block_source[:, 0].reshape(N_FRAME, NB).astype(jnp.int32)
    earlier = jnp.arange(NB)[None, :] < jnp.arange(NB)[:, None]
    ranked = lax.optimization_barrier(jnp.sum(((source[:, :, None] == source[:, None, :]) & earlier[None]).astype(jnp.int32), axis=2)).astype(jnp.int32)
    frames = jnp.arange(N_FRAME, dtype=jnp.int32)[:, None]
    offset = block_slot[frames, source, ranked].astype(jnp.int32)
    chosen = ((frames * N_HEAD + source) * NB + offset).reshape(-1).astype(jnp.int32)
    patches = encoded.reshape(-1, BLK_ROWS, MEDIA)[chosen].reshape(PATCHES, MEDIA)
    normed = layer_norm(patches, media_gain)
    position = jnp.arange(PATCHES, dtype=jnp.int32)
    bounds = jnp.cumsum(video_patches).astype(jnp.int32)
    patch_video = lax.optimization_barrier(jnp.sum((position[:, None] >= bounds[None, :]).astype(jnp.int32), axis=1)).astype(jnp.int32)
    row_video = jnp.repeat(latent_video, LAT_BLK).astype(jnp.int32)
    allowed = row_video[:, None] == patch_video[None, :]
    scale = HEAD_DIM ** (-0.5)

    def one_head(head):
        start = head * HEAD_DIM
        keys = jnp.dot(normed, lax.dynamic_slice_in_dim(w_key, start, HEAD_DIM, 1), preferred_element_type=jnp.float32).astype(jnp.bfloat16)
        values = jnp.dot(normed, lax.dynamic_slice_in_dim(w_value, start, HEAD_DIM, 1), preferred_element_type=jnp.float32).astype(jnp.bfloat16)
        query_cols = lax.dynamic_slice_in_dim(queries, start, HEAD_DIM, 1)
        scores = lax.dot_general(query_cols, keys, (((1,), (1,)), ((), ())), preferred_element_type=jnp.float32) * scale
        masked = jnp.where(allowed, scores, -1e+30)
        top = lax.optimization_barrier(jnp.max(masked, axis=1))
        weights = jnp.where(allowed, jnp.exp(masked - top[:, None]), 0.0)
        total = lax.optimization_barrier(jnp.sum(weights, axis=1))
        numer = jnp.dot(weights.astype(jnp.bfloat16), values, preferred_element_type=jnp.float32)
        return (numer / total[:, None]).astype(jnp.bfloat16)
    heads_out = lax.map(one_head, jnp.arange(HEADS, dtype=jnp.int32))
    return jnp.transpose(heads_out, (1, 0, 2)).reshape(LAT, D)
```

```python
import functools
import math

import jax
import jax.numpy as jnp
from jax import lax
from jax.experimental import pallas as pl
from jax.experimental.pallas import tpu as pltpu
from jax.sharding import Mesh, PartitionSpec as P

HEAD_DIM = 128
LAT_BLK = 2
BLK = 128
NB = 4
MEDIA = 1152
LAT = 768
NUM_LAT = 256
VIDEOS = 3
NX, NY, NZ = 4, 4, 8
PAIR = 2
HEADS_HERE = 4
COLS = HEADS_HERE * HEAD_DIM
WIDE = COLS + 128
ROWS = PAIR * NB * BLK
OWN = 6
SCALE2 = HEAD_DIM ** (-0.5) * math.log2(math.e)
EMPTY = -1e30
VMEM = pl.BlockSpec(memory_space=pltpu.VMEM)
SMEM = pl.BlockSpec(memory_space=pltpu.SMEM)


def norm_kernel(slot_ref, rows_ref, gain_ref, out_ref):
    values = rows_ref[0].astype(jnp.float32)
    center = values - jnp.mean(values, axis=1, keepdims=True)
    spread = jnp.mean(center * center, axis=1, keepdims=True)
    out_ref[0] = (center * lax.rsqrt(spread + 1e-6) * gain_ref[...]).astype(jnp.bfloat16)


def norm_slots(slots, blocks, media_gain):
    return pl.pallas_call(
        norm_kernel,
        grid_spec=pltpu.PrefetchScalarGridSpec(
            num_scalar_prefetch=1,
            grid=(2,),
            in_specs=[
                pl.BlockSpec((1, BLK, MEDIA), lambda i, s: (s[i], 0, 0)),
                pl.BlockSpec((1, MEDIA), lambda i, s: (0, 0)),
            ],
            out_specs=pl.BlockSpec((1, BLK, MEDIA), lambda i, s: (i, 0, 0)),
        ),
        out_shape=jax.ShapeDtypeStruct((2, BLK, MEDIA), jnp.bfloat16),
        name="norm_slots",
    )(slots, blocks, media_gain.reshape(1, MEDIA))


def split_words(value):
    high = value.astype(jnp.bfloat16).astype(jnp.float32)
    return high, value - high


def lay_words(lane, head, top, total, extras):
    for k, word in enumerate((*split_words(top), *split_words(total))):
        extras = jnp.where(lane == 4 * head + k, word, extras)
    return extras


def attend_kernel(info_ref, mine_ref, other_ref, wk_ref, wv_ref, q_ref, place_row_ref, place_col_ref, out_ref, rows, acc, sem):
    def copy(b, src):
        return pltpu.make_async_copy(
            src.at[info_ref[8 + b]], rows.at[pl.ds(b * BLK, BLK)], sem.at[b]
        )

    for b in range(PAIR * NB):
        @pl.when(info_ref[b] == 0)
        def _():
            copy(b, mine_ref).start()

        @pl.when(info_ref[b] != 0)
        def _():
            copy(b, other_ref).start()
    acc[...] = jnp.zeros_like(acc)
    for b in range(PAIR * NB):
        copy(b, mine_ref).wait()
    x = rows[...]
    keys = jnp.dot(x, wk_ref[...], preferred_element_type=jnp.float32).astype(jnp.bfloat16)
    values = jnp.dot(x, wv_ref[...], preferred_element_type=jnp.float32).astype(jnp.bfloat16)
    base = info_ref[16]
    ends = (info_ref[17], info_ref[18], info_ref[19])
    position = base + lax.broadcasted_iota(jnp.int32, (1, ROWS), 1)
    for v in range(VIDEOS):
        first = 0 if v == 0 else ends[v - 1]
        last = ends[v]

        @pl.when((first < base + ROWS) & (last > base) & (first < last))
        def _():
            allowed = (position >= first) & (position < last)
            pick = (
                place_row_ref[...] == v * NUM_LAT + lax.broadcasted_iota(jnp.int32, (NUM_LAT, LAT), 0)
            ).astype(jnp.bfloat16)
            put = (
                place_col_ref[...] == v * NUM_LAT + lax.broadcasted_iota(jnp.int32, (LAT, NUM_LAT), 1)
            ).astype(jnp.bfloat16)
            queries = jnp.dot(pick, q_ref[...], preferred_element_type=jnp.float32).astype(jnp.bfloat16)
            lane = lax.broadcasted_iota(jnp.int32, (NUM_LAT, 128), 1)
            extras = jnp.zeros((NUM_LAT, 128), jnp.float32)
            for h in range(HEADS_HERE):
                cols = slice(h * HEAD_DIM, (h + 1) * HEAD_DIM)
                scores = lax.dot_general(
                    queries[:, cols],
                    keys[:, cols],
                    (((1,), (1,)), ((), ())),
                    preferred_element_type=jnp.float32,
                ) * SCALE2
                scores = jnp.where(allowed, scores, EMPTY)
                high, low = split_words(jnp.max(scores, axis=1, keepdims=True))
                top = high + low.astype(jnp.bfloat16).astype(jnp.float32)
                weights = jnp.where(allowed, jnp.exp2(scores - top), 0.0)
                total = jnp.sum(weights, axis=1, keepdims=True)
                numer = jnp.dot(
                    weights.astype(jnp.bfloat16), values[:, cols], preferred_element_type=jnp.float32
                )
                extras = lay_words(lane, h, top, total, extras)
                acc[:, cols] += jnp.dot(put, numer.astype(jnp.bfloat16), preferred_element_type=jnp.float32)
            acc[:, COLS:] += jnp.dot(put, extras.astype(jnp.bfloat16), preferred_element_type=jnp.float32)

    out_ref[...] = acc[...].astype(jnp.bfloat16)


def attend(info, mine, other, wk, wv, q, place):
    return pl.pallas_call(
        attend_kernel,
        in_specs=[SMEM, pl.BlockSpec(memory_space=pl.ANY), pl.BlockSpec(memory_space=pl.ANY)] + [VMEM] * 5,
        out_specs=VMEM,
        out_shape=jax.ShapeDtypeStruct((LAT, WIDE), jnp.bfloat16),
        scratch_shapes=[
            pltpu.VMEM((ROWS, MEDIA), jnp.bfloat16),
            pltpu.VMEM((LAT, WIDE), jnp.float32),
            pltpu.SemaphoreType.DMA((PAIR * NB,)),
        ],
        compiler_params=pltpu.CompilerParams(vmem_limit_bytes=48 * 1024 * 1024),
        name="attend",
    )(info, mine, other, wk, wv, q, place.reshape(1, LAT), place.reshape(LAT, 1))


def gather_words(extras, head):
    top = extras[..., 4 * head:4 * head + 1] + extras[..., 4 * head + 1:4 * head + 2]
    total = extras[..., 4 * head + 2:4 * head + 3] + extras[..., 4 * head + 3:4 * head + 4]
    return jnp.where(total > 0, top, EMPTY), total


def merge_kernel(parts_ref, out_ref):
    rows = LAT // NX
    lane = lax.broadcasted_iota(jnp.int32, (rows, 128), 1)
    extras_in = parts_ref[:, :, COLS:].astype(jnp.float32)
    extras = jnp.zeros((rows, 128), jnp.float32)
    spread_rows = NY * NZ * 8
    target = lax.broadcasted_iota(jnp.int32, (spread_rows, rows), 0)
    source = lax.broadcasted_iota(jnp.int32, (spread_rows, rows), 1)
    put = ((target // 8 * OWN + target % 8 == source) & (target % 8 < OWN)).astype(jnp.bfloat16)
    for h in range(HEADS_HERE):
        cols = slice(h * HEAD_DIM, (h + 1) * HEAD_DIM)
        top, total = gather_words(extras_in, h)
        best = jnp.max(top, axis=0)
        factor = jnp.where(total > 0, jnp.exp2(top - best[None]), 0.0)
        whole = jnp.sum(total * factor, axis=0)
        numer = jnp.sum(parts_ref[:, :, cols].astype(jnp.float32) * factor, axis=0)
        extras = lay_words(lane, h, jnp.where(whole > 0, best, 0.0), whole, extras)
        moved = jnp.dot(put, numer.astype(jnp.bfloat16), preferred_element_type=jnp.float32)
        out_ref[:, :, cols] = moved.astype(jnp.bfloat16).reshape(NY * NZ, 8, HEAD_DIM)
    moved = jnp.dot(put, extras.astype(jnp.bfloat16), preferred_element_type=jnp.float32)
    out_ref[:, :, COLS:] = moved.astype(jnp.bfloat16).reshape(NY * NZ, 8, 128)


def merge(parts):
    return pl.pallas_call(
        merge_kernel,
        in_specs=[VMEM],
        out_specs=VMEM,
        out_shape=jax.ShapeDtypeStruct((NY * NZ, 8, WIDE), jnp.bfloat16),
        name="merge",
    )(parts)


def finish_kernel(parts_ref, out_ref):
    groups = NY * NZ // PAIR
    for part in range(PAIR):
        extras = parts_ref[:, part, :, COLS:].astype(jnp.float32)
        for h in range(HEADS_HERE):
            cols = slice(h * HEAD_DIM, (h + 1) * HEAD_DIM)
            top, total = gather_words(extras, h)
            best = jnp.max(top, axis=0)
            factor = jnp.where(total > 0, jnp.exp2(top - best[None]), 0.0)
            whole = jnp.sum(total * factor, axis=0)
            numer = jnp.sum(parts_ref[:, part, :, cols].astype(jnp.float32) * factor, axis=0)
            result = (numer / whole).astype(jnp.bfloat16)
            start = part * COLS + h * HEAD_DIM
            out_ref[:, start:start + HEAD_DIM] = result[:OWN]


def finish(parts):
    return pl.pallas_call(
        finish_kernel,
        in_specs=[VMEM],
        out_specs=VMEM,
        out_shape=jax.ShapeDtypeStruct((OWN, PAIR * COLS), jnp.bfloat16),
        name="finish",
    )(parts.reshape(NY * NZ // PAIR, PAIR, 8, WIDE))


def exchange(value, axis):
    return lax.all_to_all(value, axis, split_axis=0, concat_axis=0, tiled=True)


def spread(value, axis, count):
    return exchange(jnp.broadcast_to(value[None], (count,) + value.shape), axis)


def shards(
    encoded,
    block_source,
    block_slot,
    video_patches,
    latent_video,
    media_gain,
    queries,
    w_key,
    w_value,
):
    ax, ay, az = lax.axis_index("x"), lax.axis_index("yh"), lax.axis_index("z")
    al, ac = lax.axis_index("yl"), lax.axis_index("c")
    head = al * 2 + ac
    swap_z = [(i, i ^ 1) for i in range(NZ)]
    swap = [(0, 1), (1, 0)]

    slot = lax.dynamic_index_in_dim(block_slot[0], head, 0, keepdims=False)[:2]
    own = norm_slots(slot, encoded.reshape(NB, BLK, MEDIA), media_gain)
    near_y = lax.ppermute(own, "yl", swap)
    near_z = lax.ppermute(own, "z", swap_z)
    source_z = lax.ppermute(block_source, "z", swap_z)

    local = jnp.concatenate([w_key, w_value, queries], axis=0)
    rows = local.shape[0]
    local = jnp.transpose(local.reshape(rows, PAIR, COLS), (1, 0, 2))
    line = exchange(jnp.tile(local, (NZ // PAIR, 1, 1)), "z")
    line = jnp.concatenate(
        [line[:, :9].reshape(72, COLS), line[:, 9:18].reshape(72, COLS), line[:, 18:].reshape(48, COLS)], axis=0
    )
    far_y = lax.ppermute(near_z[0:1], "yl", swap)
    far_z = lax.ppermute(near_y[1:2], "z", swap_z)
    plane = spread(line, "yh", NY)
    plane_k = plane[:, :72].reshape(288, COLS)
    plane_v = plane[:, 72:144].reshape(288, COLS)
    plane_q = plane[:, 144:].reshape(192, COLS)
    mine = jnp.concatenate([own, near_y, near_z, far_y, far_z], axis=0)
    other = lax.ppermute(mine, "c", swap)
    cube = spread(jnp.concatenate([plane_k, plane_q, plane_v], axis=0), "x", NX)
    wk = cube[:, :288].reshape(MEDIA, COLS)
    q = cube[:, 288:480].reshape(LAT, COLS)
    wv = cube[:, 480:].reshape(MEDIA, COLS)

    part = az % PAIR
    pair_source = jnp.where(
        part == 0,
        jnp.concatenate([block_source[:, 0], source_z[:, 0]]),
        jnp.concatenate([source_z[:, 0], block_source[:, 0]]),
    )
    block = jnp.arange(PAIR * NB, dtype=jnp.int32)
    same = (pair_source[:, None] == pair_source[None, :]) & (block[None, :] < block[:, None])
    same = same & (block[:, None] // NB == block[None, :] // NB)
    rank = jnp.sum(same.astype(jnp.int32), axis=1)
    place_in = ((block // NB) ^ part) * 4 + ((pair_source // 2) ^ al) * 2 + rank
    ends = jnp.cumsum(video_patches)
    base = (ax * (NY * NZ) + ay * NZ + az - part) * (NB * BLK)
    info = jnp.concatenate(
        [(pair_source % 2) ^ ac, place_in, base[None].astype(jnp.int32), ends.astype(jnp.int32)]
    ).astype(jnp.int32)

    which = (latent_video[:, None] == jnp.arange(VIDEOS)[None, :]).astype(jnp.int32)
    before = jnp.cumsum(which, axis=0) - which
    block_place = latent_video * NUM_LAT + LAT_BLK * jnp.sum(before * which, axis=1)
    place = (block_place[:, None] + jnp.arange(LAT_BLK)[None, :]).reshape(-1).astype(jnp.int32)

    message = attend(info, mine, other, wk, wv, q, place)
    merged = merge(exchange(message.reshape(NX, LAT // NX, WIDE), "x"))
    return finish(exchange(merged, ("yh", "z")))


def solution(mesh):
    grid = Mesh(mesh.devices.reshape(NX, NY, NZ, 2, 2), ("x", "yh", "z", "yl", "c"))
    frame, head = ("x", "yh", "z"), ("yl", "c")
    placed = (
        P(frame + head, None),
        P(frame, None),
        P(frame, None, None),
        P(),
        P(),
        P(),
        P(frame, head),
        P(frame, head),
        P(frame, head),
    )
    return jax.shard_map(
        shards, mesh=grid, in_specs=placed, out_specs=P(frame, head), check_vma=False
    )
```

```python
import functools
import math

import jax
import jax.numpy as jnp
from jax import lax
from jax.experimental import pallas as pl
from jax.experimental.pallas import tpu as pltpu
from jax.sharding import Mesh, PartitionSpec as P

HEAD_DIM = 128
LAT_BLK = 2
BLK = 128
NB = 4
MEDIA = 1152
LAT = 768
NUM_LAT = 256
VIDEOS = 3
NX, NY, NZ = 4, 4, 8
PARTS = 4
HEADS_HERE = 2
COLS = HEADS_HERE * HEAD_DIM
PADDED = 128 * 8
FRAME_ROWS = NB * BLK
ROWS = PARTS * FRAME_ROWS
BLOCKS = PARTS * NB
RING = 8
OWN = 6
SCALE2 = HEAD_DIM ** (-0.5) * math.log2(math.e)
EMPTY = -1e30
VMEM = pl.BlockSpec(memory_space=pltpu.VMEM)
SMEM = pl.BlockSpec(memory_space=pltpu.SMEM)


def norm_kernel(slot_ref, rows_ref, gain_ref, out_ref):
    values = rows_ref[0].astype(jnp.float32)
    center = values - jnp.mean(values, axis=1, keepdims=True)
    spread = jnp.mean(center * center, axis=1, keepdims=True)
    out_ref[0] = (center * lax.rsqrt(spread + 1e-6) * gain_ref[...][None, :]).astype(jnp.bfloat16)


def norm_slots(slots, blocks, media_gain):
    return pl.pallas_call(
        norm_kernel,
        grid_spec=pltpu.PrefetchScalarGridSpec(
            num_scalar_prefetch=1,
            grid=(2,),
            in_specs=[
                pl.BlockSpec((1, BLK, MEDIA), lambda i, s: (s[i], 0, 0)),
                pl.BlockSpec((MEDIA,), lambda i, s: (0,)),
            ],
            out_specs=pl.BlockSpec((1, BLK, MEDIA), lambda i, s: (i, 0, 0)),
        ),
        out_shape=jax.ShapeDtypeStruct((2, BLK, MEDIA), jnp.bfloat16),
        name="norm_slots",
    )(slots, blocks, media_gain)


def split_words(value):
    high = value.astype(jnp.bfloat16).astype(jnp.float32)
    return high, value - high


def lay_words(lane, head, top, total, extras):
    for k, word in enumerate((*split_words(top), *split_words(total))):
        extras = jnp.where(lane % 8 == 4 * head + k, word, extras)
    return extras


def attend_kernel(
    info_ref, slots_ref, cube_ref, row_ref, col_ref, out_ref, rows, keys, values, numer, state, acc, sem
):
    def copy(b):
        return pltpu.make_async_copy(slots_ref.at[info_ref[b]], rows.at[pl.ds(b * BLK, BLK)], sem.at[b])

    for b in range(BLOCKS):
        copy(b).start()
    wk = cube_ref[:, :288].reshape(MEDIA, COLS)
    wv = cube_ref[:, 288:576].reshape(MEDIA, COLS)
    every = cube_ref[:, 576:].reshape(LAT, COLS)
    acc[...] = jnp.zeros_like(acc)
    for g in range(PARTS):
        for b in range(g * NB, (g + 1) * NB):
            copy(b).wait()
        span = slice(g * FRAME_ROWS, (g + 1) * FRAME_ROWS)
        x = rows[span]
        keys[span] = jnp.dot(x, wk, preferred_element_type=jnp.float32).astype(jnp.bfloat16)
        values[span] = jnp.dot(x, wv, preferred_element_type=jnp.float32).astype(jnp.bfloat16)
    base = info_ref[BLOCKS]
    ends = [info_ref[BLOCKS + 1 + v] for v in range(VIDEOS)]
    offset = lax.broadcasted_iota(jnp.int32, (1, FRAME_ROWS), 1)
    lane = lax.broadcasted_iota(jnp.int32, (NUM_LAT, 128), 1)
    stride = NZ * FRAME_ROWS
    for v in range(VIDEOS):
        first = 0 if v == 0 else ends[v - 1]
        last = ends[v]
        seen = [
            (first < base + g * stride + FRAME_ROWS) & (last > base + g * stride) & (first < last)
            for g in range(PARTS)
        ]

        @pl.when(seen[0] | seen[1] | seen[2] | seen[3])
        def _():
            pick = (
                row_ref[...] == v * NUM_LAT + lax.broadcasted_iota(jnp.int32, (NUM_LAT, LAT), 0)
            ).astype(jnp.bfloat16)
            queries = jnp.dot(pick, every, preferred_element_type=jnp.float32).astype(jnp.bfloat16)
            numer[...] = jnp.zeros_like(numer)
            for h in range(HEADS_HERE):
                state[2 * h] = jnp.full((NUM_LAT, 1), EMPTY, jnp.float32)
                state[2 * h + 1] = jnp.zeros((NUM_LAT, 1), jnp.float32)
            for g in range(PARTS):
                @pl.when(seen[g])
                def _():
                    position = base + g * stride + offset
                    allowed = (position >= first) & (position < last)
                    span = slice(g * FRAME_ROWS, (g + 1) * FRAME_ROWS)
                    for h in range(HEADS_HERE):
                        cols = slice(h * HEAD_DIM, (h + 1) * HEAD_DIM)
                        scores = lax.dot_general(
                            queries[:, cols],
                            keys[span, cols],
                            (((1,), (1,)), ((), ())),
                            preferred_element_type=jnp.float32,
                        ) * SCALE2
                        scores = jnp.where(allowed, scores, EMPTY)
                        before = state[2 * h]
                        high, low = split_words(
                            jnp.maximum(before, jnp.max(scores, axis=1, keepdims=True))
                        )
                        top = high + low.astype(jnp.bfloat16).astype(jnp.float32)
                        weights = jnp.where(allowed, jnp.exp2(scores - top), 0.0)
                        keep = jnp.where(before > EMPTY, jnp.exp2(before - top), 0.0)
                        state[2 * h] = top
                        state[2 * h + 1] = state[2 * h + 1] * keep + jnp.sum(weights, axis=1, keepdims=True)
                        numer[:, cols] = numer[:, cols] * keep + jnp.dot(
                            weights.astype(jnp.bfloat16), values[span, cols], preferred_element_type=jnp.float32
                        )
            put = (
                col_ref[...] == v * NUM_LAT + lax.broadcasted_iota(jnp.int32, (PADDED, NUM_LAT), 1)
            ).astype(jnp.bfloat16)
            extras = jnp.zeros((NUM_LAT, 128), jnp.float32)
            for h in range(HEADS_HERE):
                extras = lay_words(lane, h, state[2 * h], state[2 * h + 1], extras)
            acc[:, :COLS] += jnp.dot(put, numer[...].astype(jnp.bfloat16), preferred_element_type=jnp.float32)
            acc[:, COLS:] += jnp.dot(put, extras.astype(jnp.bfloat16), preferred_element_type=jnp.float32)

    words = acc[:, COLS:].reshape(PADDED // 8, 8, 128)
    row = lax.broadcasted_iota(jnp.int32, words.shape, 1)
    group = lax.broadcasted_iota(jnp.int32, words.shape, 2) // 8
    words = jnp.sum(jnp.where(row == group, words, 0.0), axis=1, keepdims=True)
    sums = acc[:, :128].reshape(PADDED // 8, 8, 128)
    out_ref[:, :128] = jnp.where(row == OWN, words, sums).reshape(PADDED, 128).astype(jnp.bfloat16)
    out_ref[:, 128:] = acc[:, 128:COLS].astype(jnp.bfloat16)


def attend(info, slots, cube, place, target):
    return pl.pallas_call(
        attend_kernel,
        in_specs=[SMEM] + [pl.BlockSpec(memory_space=pl.ANY)] + [VMEM] * 3,
        out_specs=VMEM,
        out_shape=jax.ShapeDtypeStruct((PADDED, COLS), jnp.bfloat16),
        scratch_shapes=[
            pltpu.VMEM((ROWS, MEDIA), jnp.bfloat16),
            pltpu.VMEM((ROWS, COLS), jnp.bfloat16),
            pltpu.VMEM((ROWS, COLS), jnp.bfloat16),
            pltpu.VMEM((NUM_LAT, COLS), jnp.float32),
            pltpu.VMEM((2 * HEADS_HERE, NUM_LAT, 1), jnp.float32),
            pltpu.VMEM((PADDED, COLS + 128), jnp.float32),
            pltpu.SemaphoreType.DMA((BLOCKS,)),
        ],
        compiler_params=pltpu.CompilerParams(vmem_limit_bytes=48 * 1024 * 1024),
        name="attend",
    )(info, slots, cube, place.reshape(1, LAT), target.reshape(PADDED, 1))


def arrange_kernel(rows_ref, out_ref):
    count = NY * NZ * 24
    to = lax.broadcasted_iota(jnp.int32, (count, 1), 0)
    key = jnp.where(to < 288, to, to - 288)
    pair = key // 9 * 24 + key % 9 + jnp.where(to < 288, 0, 9)
    query = to - 576
    pick = jnp.where(to < 576, pair, query // OWN * 24 + query % OWN + 18)
    move = (pick == lax.broadcasted_iota(jnp.int32, (count, count), 1)).astype(jnp.bfloat16)
    rows = jnp.dot(move, rows_ref[...], preferred_element_type=jnp.float32).astype(jnp.bfloat16)
    for i in range(NX):
        out_ref[i] = rows


def arrange(rows):
    return pl.pallas_call(
        arrange_kernel,
        in_specs=[VMEM],
        out_specs=VMEM,
        out_shape=jax.ShapeDtypeStruct((NX, NY * NZ * 24, COLS), jnp.bfloat16),
        compiler_params=pltpu.CompilerParams(vmem_limit_bytes=32 * 1024 * 1024),
        name="arrange",
    )(rows.reshape(NY * NZ * 24, COLS))


def finish_kernel(parts_ref, out_ref):
    shape = (NX, NZ, 8, HEAD_DIM)
    lane = lax.broadcasted_iota(jnp.int32, shape, 3)
    row = lax.broadcasted_iota(jnp.int32, shape, 2)
    for part in range(PARTS):
        words = parts_ref[:, part, :, OWN:OWN + 1, :128].astype(jnp.float32)
        for h in range(HEADS_HERE):
            cols = slice(h * HEAD_DIM, (h + 1) * HEAD_DIM)
            at = lane - (8 * row + 4 * h)
            top = jnp.sum(jnp.where((at == 0) | (at == 1), words, 0.0), axis=3, keepdims=True)
            total = jnp.sum(jnp.where((at == 2) | (at == 3), words, 0.0), axis=3, keepdims=True)
            top = jnp.where(total > 0, top, EMPTY)
            best = jnp.max(top, axis=(0, 1), keepdims=True)
            factor = jnp.where(total > 0, jnp.exp2(top - best), 0.0)
            whole = jnp.sum(total * factor, axis=(0, 1))
            numer = jnp.sum(parts_ref[:, part, :, :, cols].astype(jnp.float32) * factor, axis=(0, 1))
            result = (numer / whole).astype(jnp.bfloat16)
            start = part * COLS + h * HEAD_DIM
            out_ref[:, start:start + HEAD_DIM] = result[:OWN]


def finish(parts):
    return pl.pallas_call(
        finish_kernel,
        in_specs=[VMEM],
        out_specs=VMEM,
        out_shape=jax.ShapeDtypeStruct((OWN, PARTS * COLS), jnp.bfloat16),
        compiler_params=pltpu.CompilerParams(vmem_limit_bytes=48 * 1024 * 1024),
        name="finish",
    )(parts.reshape(NX, NY, NZ, 8, COLS))


def exchange(value, axis):
    return lax.all_to_all(value, axis, split_axis=0, concat_axis=0, tiled=True)


def spread(value, axis, count):
    return exchange(jnp.broadcast_to(value[None], (count,) + value.shape), axis)


def shards(
    encoded,
    block_source,
    block_slot,
    video_patches,
    latent_video,
    media_gain,
    queries,
    w_key,
    w_value,
):
    ax, az = lax.axis_index("x"), lax.axis_index("z")
    al, ac = lax.axis_index("yl"), lax.axis_index("c")
    head = al * 2 + ac
    slot = lax.dynamic_index_in_dim(block_slot[0], head, 0, keepdims=False)[:2]
    own = norm_slots(slot, encoded.reshape(NB, BLK, MEDIA), media_gain)
    slots = lax.all_gather(own, ("yh", "yl", "c"), axis=0, tiled=True)
    local = jnp.concatenate([w_key, w_value, queries], axis=0)
    local = jnp.transpose(local.reshape(24, PARTS, COLS), (1, 0, 2))
    plane = exchange(jnp.repeat(local, NZ, axis=0), ("yh", "z"))
    cube = exchange(arrange(plane), "x")

    source = exchange(jnp.broadcast_to(block_source[None], (NY, NB, 1)), "yh").reshape(BLOCKS)
    block = jnp.arange(BLOCKS, dtype=jnp.int32)
    same = (source[:, None] == source[None, :]) & (block[None, :] < block[:, None])
    same = same & (block[:, None] // NB == block[None, :] // NB)
    rank = jnp.sum(same.astype(jnp.int32), axis=1)
    index = (block // NB * 4 + source) * 2 + rank
    ends = jnp.cumsum(video_patches)
    base = (ax * (NY * NZ) + az) * FRAME_ROWS
    info = jnp.concatenate([index, base[None].astype(jnp.int32), ends.astype(jnp.int32)]).astype(jnp.int32)

    which = (latent_video[:, None] == jnp.arange(VIDEOS)[None, :]).astype(jnp.int32)
    before = jnp.cumsum(which, axis=0) - which
    block_place = latent_video * NUM_LAT + LAT_BLK * jnp.sum(before * which, axis=1)
    place = (block_place[:, None] + jnp.arange(LAT_BLK)[None, :]).reshape(-1).astype(jnp.int32)

    target = jnp.pad(place.reshape(PADDED // 8, OWN), ((0, 0), (0, 8 - OWN)), constant_values=-1)
    message = attend(info, slots, cube, place, target)
    return finish(exchange(message.reshape(PADDED // 8, 8, COLS), ("x", "yh", "z")))


def solution(mesh):
    grid = Mesh(mesh.devices.reshape(NX, NY, NZ, 2, 2), ("x", "yh", "z", "yl", "c"))
    frame, head = ("x", "yh", "z"), ("yl", "c")
    placed = (
        P(frame + head, None),
        P(frame, None),
        P(frame, None, None),
        P(),
        P(),
        P(),
        P(frame, head),
        P(frame, head),
        P(frame, head),
    )
    return jax.shard_map(
        shards, mesh=grid, in_specs=placed, out_specs=P(frame, head), check_vma=False
    )
```

```python
import functools
import math

import jax
import jax.numpy as jnp
from jax import lax
from jax.experimental import pallas as pl
from jax.experimental.pallas import tpu as pltpu
from jax.sharding import Mesh, PartitionSpec as P

HEAD_DIM = 128
LAT_BLK = 2
BLK = 128
NB = 4
MEDIA = 1152
LAT = 768
NUM_LAT = 256
VIDEOS = 3
NX, NY, NZ = 4, 4, 8
PARTS = 4
HEADS_HERE = 2
COLS = HEADS_HERE * HEAD_DIM
PADDED = 128 * 8
FRAME_ROWS = NB * BLK
ROWS = PARTS * FRAME_ROWS
BLOCKS = PARTS * NB
RING = 8
OWN = 6
SCALE2 = HEAD_DIM ** (-0.5) * math.log2(math.e)
EMPTY = -1e30
VMEM = pl.BlockSpec(memory_space=pltpu.VMEM)
SMEM = pl.BlockSpec(memory_space=pltpu.SMEM)


def norm_kernel(slot_ref, rows_ref, gain_ref, out_ref):
    values = rows_ref[0].astype(jnp.float32)
    center = values - jnp.mean(values, axis=1, keepdims=True)
    spread = jnp.mean(center * center, axis=1, keepdims=True)
    out_ref[0] = (center * lax.rsqrt(spread + 1e-6) * gain_ref[...][None, :]).astype(jnp.bfloat16)


def norm_slots(slots, blocks, media_gain):
    return pl.pallas_call(
        norm_kernel,
        grid_spec=pltpu.PrefetchScalarGridSpec(
            num_scalar_prefetch=1,
            grid=(2,),
            in_specs=[
                pl.BlockSpec((1, BLK, MEDIA), lambda i, s: (s[i], 0, 0)),
                pl.BlockSpec((MEDIA,), lambda i, s: (0,)),
            ],
            out_specs=pl.BlockSpec((1, BLK, MEDIA), lambda i, s: (i, 0, 0)),
        ),
        out_shape=jax.ShapeDtypeStruct((2, BLK, MEDIA), jnp.bfloat16),
        name="norm_slots",
    )(slots, blocks, media_gain)


def split_words(value):
    high = value.astype(jnp.bfloat16).astype(jnp.float32)
    return high, value - high


def lay_words(lane, head, top, total, extras):
    for k, word in enumerate((*split_words(top), *split_words(total))):
        extras = jnp.where(lane % 8 == 4 * head + k, word, extras)
    return extras


def attend_kernel(
    info_ref, slots_ref, cube_ref, row_ref, col_ref, out_ref, rows, keys, values, numer, state, acc, sem
):
    def copy(b):
        return pltpu.make_async_copy(slots_ref.at[info_ref[b]], rows.at[pl.ds(b * BLK, BLK)], sem.at[b])

    for b in range(BLOCKS):
        copy(b).start()
    wk = cube_ref[:, :288].reshape(MEDIA, COLS)
    wv = cube_ref[:, 288:576].reshape(MEDIA, COLS)
    every = cube_ref[:, 576:].reshape(LAT, COLS)
    acc[...] = jnp.zeros_like(acc)
    for g in range(PARTS):
        for b in range(g * NB, (g + 1) * NB):
            copy(b).wait()
        span = slice(g * FRAME_ROWS, (g + 1) * FRAME_ROWS)
        x = rows[span]
        keys[span] = jnp.dot(x, wk, preferred_element_type=jnp.float32).astype(jnp.bfloat16)
        values[span] = jnp.dot(x, wv, preferred_element_type=jnp.float32).astype(jnp.bfloat16)
    base = info_ref[BLOCKS]
    ends = [info_ref[BLOCKS + 1 + v] for v in range(VIDEOS)]
    offset = lax.broadcasted_iota(jnp.int32, (1, FRAME_ROWS), 1)
    lane = lax.broadcasted_iota(jnp.int32, (NUM_LAT, 128), 1)
    stride = NZ * FRAME_ROWS
    for v in range(VIDEOS):
        first = 0 if v == 0 else ends[v - 1]
        last = ends[v]
        seen = [
            (first < base + g * stride + FRAME_ROWS) & (last > base + g * stride) & (first < last)
            for g in range(PARTS)
        ]

        @pl.when(seen[0] | seen[1] | seen[2] | seen[3])
        def _():
            pick = (
                row_ref[...] == v * NUM_LAT + lax.broadcasted_iota(jnp.int32, (NUM_LAT, LAT), 0)
            ).astype(jnp.bfloat16)
            queries = jnp.dot(pick, every, preferred_element_type=jnp.float32).astype(jnp.bfloat16)
            numer[...] = jnp.zeros_like(numer)
            for h in range(HEADS_HERE):
                state[2 * h] = jnp.full((NUM_LAT, 1), EMPTY, jnp.float32)
                state[2 * h + 1] = jnp.zeros((NUM_LAT, 1), jnp.float32)
            for g in range(PARTS):
                @pl.when(seen[g])
                def _():
                    position = base + g * stride + offset
                    allowed = (position >= first) & (position < last)
                    span = slice(g * FRAME_ROWS, (g + 1) * FRAME_ROWS)
                    for h in range(HEADS_HERE):
                        cols = slice(h * HEAD_DIM, (h + 1) * HEAD_DIM)
                        scores = lax.dot_general(
                            queries[:, cols],
                            keys[span, cols],
                            (((1,), (1,)), ((), ())),
                            preferred_element_type=jnp.float32,
                        ) * SCALE2
                        scores = jnp.where(allowed, scores, EMPTY)
                        before = state[2 * h]
                        high, low = split_words(
                            jnp.maximum(before, jnp.max(scores, axis=1, keepdims=True))
                        )
                        top = high + low.astype(jnp.bfloat16).astype(jnp.float32)
                        weights = jnp.where(allowed, jnp.exp2(scores - top), 0.0)
                        keep = jnp.where(before > EMPTY, jnp.exp2(before - top), 0.0)
                        state[2 * h] = top
                        state[2 * h + 1] = state[2 * h + 1] * keep + jnp.sum(weights, axis=1, keepdims=True)
                        numer[:, cols] = numer[:, cols] * keep + jnp.dot(
                            weights.astype(jnp.bfloat16), values[span, cols], preferred_element_type=jnp.float32
                        )
            put = (
                col_ref[...] == v * NUM_LAT + lax.broadcasted_iota(jnp.int32, (PADDED, NUM_LAT), 1)
            ).astype(jnp.bfloat16)
            extras = jnp.zeros((NUM_LAT, 128), jnp.float32)
            for h in range(HEADS_HERE):
                extras = lay_words(lane, h, state[2 * h], state[2 * h + 1], extras)
            acc[:, :COLS] += jnp.dot(put, numer[...].astype(jnp.bfloat16), preferred_element_type=jnp.float32)
            acc[:, COLS:] += jnp.dot(put, extras.astype(jnp.bfloat16), preferred_element_type=jnp.float32)

    words = acc[:, COLS:].reshape(PADDED // 8, 8, 128)
    row = lax.broadcasted_iota(jnp.int32, words.shape, 1)
    group = lax.broadcasted_iota(jnp.int32, words.shape, 2) // 8
    words = jnp.sum(jnp.where(row == group, words, 0.0), axis=1, keepdims=True)
    sums = acc[:, :128].reshape(PADDED // 8, 8, 128)
    out_ref[:, :128] = jnp.where(row == OWN, words, sums).reshape(PADDED, 128).astype(jnp.bfloat16)
    out_ref[:, 128:] = acc[:, 128:COLS].astype(jnp.bfloat16)


def attend(info, slots, cube, place, target):
    return pl.pallas_call(
        attend_kernel,
        in_specs=[SMEM] + [pl.BlockSpec(memory_space=pl.ANY)] + [VMEM] * 3,
        out_specs=VMEM,
        out_shape=jax.ShapeDtypeStruct((PADDED, COLS), jnp.bfloat16),
        scratch_shapes=[
            pltpu.VMEM((ROWS, MEDIA), jnp.bfloat16),
            pltpu.VMEM((ROWS, COLS), jnp.bfloat16),
            pltpu.VMEM((ROWS, COLS), jnp.bfloat16),
            pltpu.VMEM((NUM_LAT, COLS), jnp.float32),
            pltpu.VMEM((2 * HEADS_HERE, NUM_LAT, 1), jnp.float32),
            pltpu.VMEM((PADDED, COLS + 128), jnp.float32),
            pltpu.SemaphoreType.DMA((BLOCKS,)),
        ],
        compiler_params=pltpu.CompilerParams(vmem_limit_bytes=48 * 1024 * 1024),
        name="attend",
    )(info, slots, cube, place.reshape(1, LAT), target.reshape(PADDED, 1))


def arrange_kernel(rows_ref, out_ref):
    count = NY * NZ * 24
    to = lax.broadcasted_iota(jnp.int32, (count, 1), 0)
    key = jnp.where(to < 288, to, to - 288)
    query = to - 576
    frame = jnp.where(to < 576, key // 9, query // OWN)
    row = jnp.where(to < 576, key % 9 + jnp.where(to < 288, 0, 9), query % OWN + 18)
    pick = (frame % NZ * NY + frame // NZ) * 24 + row
    move = (pick == lax.broadcasted_iota(jnp.int32, (count, count), 1)).astype(jnp.bfloat16)
    rows = jnp.dot(move, rows_ref[...], preferred_element_type=jnp.float32).astype(jnp.bfloat16)
    for i in range(NX):
        out_ref[i] = rows


def arrange(rows):
    return pl.pallas_call(
        arrange_kernel,
        in_specs=[VMEM],
        out_specs=VMEM,
        out_shape=jax.ShapeDtypeStruct((NX, NY * NZ * 24, COLS), jnp.bfloat16),
        compiler_params=pltpu.CompilerParams(vmem_limit_bytes=32 * 1024 * 1024),
        name="arrange",
    )(rows.reshape(NY * NZ * 24, COLS))


def finish_kernel(parts_ref, out_ref):
    shape = (NX, NZ, 8, HEAD_DIM)
    lane = lax.broadcasted_iota(jnp.int32, shape, 3)
    row = lax.broadcasted_iota(jnp.int32, shape, 2)
    for part in range(PARTS):
        words = parts_ref[:, part, :, OWN:OWN + 1, :128].astype(jnp.float32)
        for h in range(HEADS_HERE):
            cols = slice(h * HEAD_DIM, (h + 1) * HEAD_DIM)
            at = lane - (8 * row + 4 * h)
            top = jnp.sum(jnp.where((at == 0) | (at == 1), words, 0.0), axis=3, keepdims=True)
            total = jnp.sum(jnp.where((at == 2) | (at == 3), words, 0.0), axis=3, keepdims=True)
            top = jnp.where(total > 0, top, EMPTY)
            best = jnp.max(top, axis=(0, 1), keepdims=True)
            factor = jnp.where(total > 0, jnp.exp2(top - best), 0.0)
            whole = jnp.sum(total * factor, axis=(0, 1))
            numer = jnp.sum(parts_ref[:, part, :, :, cols].astype(jnp.float32) * factor, axis=(0, 1))
            result = (numer / whole).astype(jnp.bfloat16)
            start = part * COLS + h * HEAD_DIM
            out_ref[:, start:start + HEAD_DIM] = result[:OWN]


def finish(parts):
    return pl.pallas_call(
        finish_kernel,
        in_specs=[VMEM],
        out_specs=VMEM,
        out_shape=jax.ShapeDtypeStruct((OWN, PARTS * COLS), jnp.bfloat16),
        compiler_params=pltpu.CompilerParams(vmem_limit_bytes=48 * 1024 * 1024),
        name="finish",
    )(parts.reshape(NX, NY, NZ, 8, COLS))


def exchange(value, axis):
    return lax.all_to_all(value, axis, split_axis=0, concat_axis=0, tiled=True)


def spread(value, axis, count):
    return exchange(jnp.broadcast_to(value[None], (count,) + value.shape), axis)


def shards(
    encoded,
    block_source,
    block_slot,
    video_patches,
    latent_video,
    media_gain,
    queries,
    w_key,
    w_value,
):
    ax, az = lax.axis_index("x"), lax.axis_index("z")
    al, ac = lax.axis_index("yl"), lax.axis_index("c")
    head = al * 2 + ac
    slot = lax.dynamic_index_in_dim(block_slot[0], head, 0, keepdims=False)[:2]
    own = norm_slots(slot, encoded.reshape(NB, BLK, MEDIA), media_gain)
    slots = lax.all_gather(own, ("yh", "yl", "c"), axis=0, tiled=True)
    local = jnp.concatenate([w_key, w_value, queries], axis=0)
    local = jnp.transpose(local.reshape(24, PARTS, COLS), (1, 0, 2))
    note = jnp.pad(block_source.reshape(1, NB).astype(jnp.bfloat16), ((0, 7), (0, COLS - NB)))
    local = jnp.concatenate([local, jnp.broadcast_to(note[None], (PARTS, 8, COLS))], axis=1)
    column = exchange(local, "yh")
    cube = exchange(arrange(spread(column[:, :24], "z", NZ)), "x")

    source = column[:, 24, :NB].astype(jnp.int32).reshape(BLOCKS)
    block = jnp.arange(BLOCKS, dtype=jnp.int32)
    same = (source[:, None] == source[None, :]) & (block[None, :] < block[:, None])
    same = same & (block[:, None] // NB == block[None, :] // NB)
    rank = jnp.sum(same.astype(jnp.int32), axis=1)
    index = (block // NB * 4 + source) * 2 + rank
    ends = jnp.cumsum(video_patches)
    base = (ax * (NY * NZ) + az) * FRAME_ROWS
    info = jnp.concatenate([index, base[None].astype(jnp.int32), ends.astype(jnp.int32)]).astype(jnp.int32)

    which = (latent_video[:, None] == jnp.arange(VIDEOS)[None, :]).astype(jnp.int32)
    before = jnp.cumsum(which, axis=0) - which
    block_place = latent_video * NUM_LAT + LAT_BLK * jnp.sum(before * which, axis=1)
    place = (block_place[:, None] + jnp.arange(LAT_BLK)[None, :]).reshape(-1).astype(jnp.int32)

    target = jnp.pad(place.reshape(PADDED // 8, OWN), ((0, 0), (0, 8 - OWN)), constant_values=-1)
    message = attend(info, slots, cube, place, target)
    return finish(exchange(message.reshape(PADDED // 8, 8, COLS), ("x", "yh", "z")))


def solution(mesh):
    grid = Mesh(mesh.devices.reshape(NX, NY, NZ, 2, 2), ("x", "yh", "z", "yl", "c"))
    frame, head = ("x", "yh", "z"), ("yl", "c")
    placed = (
        P(frame + head, None),
        P(frame, None),
        P(frame, None, None),
        P(),
        P(),
        P(),
        P(frame, head),
        P(frame, head),
        P(frame, head),
    )
    return jax.shard_map(
        shards, mesh=grid, in_specs=placed, out_specs=P(frame, head), check_vma=False
    )
```

```python
import functools
import math

import jax
import jax.numpy as jnp
from jax import lax
from jax.experimental import pallas as pl
from jax.experimental.pallas import tpu as pltpu
from jax.sharding import Mesh, PartitionSpec as P

HEAD_DIM = 128
LAT_BLK = 2
BLK = 128
NB = 4
MEDIA = 1152
LAT = 768
NUM_LAT = 256
VIDEOS = 3
NX, NY, NZ = 4, 4, 8
PARTS = 4
HEADS_HERE = 2
COLS = HEADS_HERE * HEAD_DIM
PADDED = 128 * 8
FRAME_ROWS = NB * BLK
ROWS = PARTS * FRAME_ROWS
BLOCKS = PARTS * NB
RING = 8
OWN = 6
SCALE2 = HEAD_DIM ** (-0.5) * math.log2(math.e)
EMPTY = -1e30
VMEM = pl.BlockSpec(memory_space=pltpu.VMEM)
SMEM = pl.BlockSpec(memory_space=pltpu.SMEM)


def norm_kernel(slot_ref, first_ref, second_ref, gain_ref, out_ref):
    for i, rows_ref in enumerate((first_ref, second_ref)):
        values = rows_ref[0].astype(jnp.float32)
        center = values - jnp.mean(values, axis=1, keepdims=True)
        spread = jnp.mean(center * center, axis=1, keepdims=True)
        out_ref[i] = (center * lax.rsqrt(spread + 1e-6) * gain_ref[...][None, :]).astype(jnp.bfloat16)


def norm_slots(slots, blocks, media_gain):
    return pl.pallas_call(
        norm_kernel,
        grid_spec=pltpu.PrefetchScalarGridSpec(
            num_scalar_prefetch=1,
            grid=(1,),
            in_specs=[
                pl.BlockSpec((1, BLK, MEDIA), lambda i, s: (s[0], 0, 0)),
                pl.BlockSpec((1, BLK, MEDIA), lambda i, s: (s[1], 0, 0)),
                pl.BlockSpec((MEDIA,), lambda i, s: (0,)),
            ],
            out_specs=pl.BlockSpec((2, BLK, MEDIA), lambda i, s: (0, 0, 0)),
        ),
        out_shape=jax.ShapeDtypeStruct((2, BLK, MEDIA), jnp.bfloat16),
        name="norm_slots",
    )(slots, blocks, blocks, media_gain)


def split_words(value):
    high = value.astype(jnp.bfloat16).astype(jnp.float32)
    return high, value - high


def lay_words(lane, head, top, total, extras):
    for k, word in enumerate((*split_words(top), *split_words(total))):
        extras = jnp.where(lane % 8 == 4 * head + k, word, extras)
    return extras


def attend_kernel(
    info_ref, slots_ref, cube_ref, row_ref, col_ref, out_ref, rows, keys, values, numer, state, acc, sem
):
    def copy(b):
        return pltpu.make_async_copy(slots_ref.at[info_ref[b]], rows.at[pl.ds(b * BLK, BLK)], sem.at[b])

    for b in range(BLOCKS):
        copy(b).start()
    wk = cube_ref[:, :288].reshape(MEDIA, COLS)
    wv = cube_ref[:, 288:576].reshape(MEDIA, COLS)
    every = cube_ref[:, 576:].reshape(LAT, COLS)
    acc[...] = jnp.zeros_like(acc)
    for g in range(PARTS):
        for b in range(g * NB, (g + 1) * NB):
            copy(b).wait()
        span = slice(g * FRAME_ROWS, (g + 1) * FRAME_ROWS)
        x = rows[span]
        keys[span] = jnp.dot(x, wk, preferred_element_type=jnp.float32).astype(jnp.bfloat16)
        values[span] = jnp.dot(x, wv, preferred_element_type=jnp.float32).astype(jnp.bfloat16)
    base = info_ref[BLOCKS]
    ends = [info_ref[BLOCKS + 1 + v] for v in range(VIDEOS)]
    offset = lax.broadcasted_iota(jnp.int32, (1, FRAME_ROWS), 1)
    lane = lax.broadcasted_iota(jnp.int32, (NUM_LAT, 128), 1)
    stride = NZ * FRAME_ROWS
    for v in range(VIDEOS):
        first = 0 if v == 0 else ends[v - 1]
        last = ends[v]
        seen = [
            (first < base + g * stride + FRAME_ROWS) & (last > base + g * stride) & (first < last)
            for g in range(PARTS)
        ]

        @pl.when(seen[0] | seen[1] | seen[2] | seen[3])
        def _():
            pick = (
                row_ref[...] == v * NUM_LAT + lax.broadcasted_iota(jnp.int32, (NUM_LAT, LAT), 0)
            ).astype(jnp.bfloat16)
            queries = jnp.dot(pick, every, preferred_element_type=jnp.float32).astype(jnp.bfloat16)
            numer[...] = jnp.zeros_like(numer)
            for h in range(HEADS_HERE):
                state[2 * h] = jnp.full((NUM_LAT, 1), EMPTY, jnp.float32)
                state[2 * h + 1] = jnp.zeros((NUM_LAT, 1), jnp.float32)
            for g in range(PARTS):
                @pl.when(seen[g])
                def _():
                    position = base + g * stride + offset
                    allowed = (position >= first) & (position < last)
                    span = slice(g * FRAME_ROWS, (g + 1) * FRAME_ROWS)
                    for h in range(HEADS_HERE):
                        cols = slice(h * HEAD_DIM, (h + 1) * HEAD_DIM)
                        scores = lax.dot_general(
                            queries[:, cols],
                            keys[span, cols],
                            (((1,), (1,)), ((), ())),
                            preferred_element_type=jnp.float32,
                        ) * SCALE2
                        scores = jnp.where(allowed, scores, EMPTY)
                        before = state[2 * h]
                        high, low = split_words(
                            jnp.maximum(before, jnp.max(scores, axis=1, keepdims=True))
                        )
                        top = high + low.astype(jnp.bfloat16).astype(jnp.float32)
                        weights = jnp.where(allowed, jnp.exp2(scores - top), 0.0)
                        keep = jnp.where(before > EMPTY, jnp.exp2(before - top), 0.0)
                        state[2 * h] = top
                        state[2 * h + 1] = state[2 * h + 1] * keep + jnp.sum(weights, axis=1, keepdims=True)
                        numer[:, cols] = numer[:, cols] * keep + jnp.dot(
                            weights.astype(jnp.bfloat16), values[span, cols], preferred_element_type=jnp.float32
                        )
            put = (
                col_ref[...] == v * NUM_LAT + lax.broadcasted_iota(jnp.int32, (PADDED, NUM_LAT), 1)
            ).astype(jnp.bfloat16)
            extras = jnp.zeros((NUM_LAT, 128), jnp.float32)
            for h in range(HEADS_HERE):
                extras = lay_words(lane, h, state[2 * h], state[2 * h + 1], extras)
            acc[:, :COLS] += jnp.dot(put, numer[...].astype(jnp.bfloat16), preferred_element_type=jnp.float32)
            acc[:, COLS:] += jnp.dot(put, extras.astype(jnp.bfloat16), preferred_element_type=jnp.float32)

    words = acc[:, COLS:].reshape(PADDED // 8, 8, 128)
    row = lax.broadcasted_iota(jnp.int32, words.shape, 1)
    group = lax.broadcasted_iota(jnp.int32, words.shape, 2) // 8
    words = jnp.sum(jnp.where(row == group, words, 0.0), axis=1, keepdims=True)
    sums = acc[:, :128].reshape(PADDED // 8, 8, 128)
    out_ref[:, :128] = jnp.where(row == OWN, words, sums).reshape(PADDED, 128).astype(jnp.bfloat16)
    out_ref[:, 128:] = acc[:, 128:COLS].astype(jnp.bfloat16)


def attend(info, slots, cube, place, target):
    return pl.pallas_call(
        attend_kernel,
        in_specs=[SMEM] + [pl.BlockSpec(memory_space=pl.ANY)] + [VMEM] * 3,
        out_specs=VMEM,
        out_shape=jax.ShapeDtypeStruct((PADDED, COLS), jnp.bfloat16),
        scratch_shapes=[
            pltpu.VMEM((ROWS, MEDIA), jnp.bfloat16),
            pltpu.VMEM((ROWS, COLS), jnp.bfloat16),
            pltpu.VMEM((ROWS, COLS), jnp.bfloat16),
            pltpu.VMEM((NUM_LAT, COLS), jnp.float32),
            pltpu.VMEM((2 * HEADS_HERE, NUM_LAT, 1), jnp.float32),
            pltpu.VMEM((PADDED, COLS + 128), jnp.float32),
            pltpu.SemaphoreType.DMA((BLOCKS,)),
        ],
        compiler_params=pltpu.CompilerParams(vmem_limit_bytes=48 * 1024 * 1024),
        name="attend",
    )(info, slots, cube, place.reshape(1, LAT), target.reshape(PADDED, 1))


def arrange_kernel(rows_ref, out_ref):
    count = NY * NZ * 24
    to = lax.broadcasted_iota(jnp.int32, (count, 1), 0)
    key = jnp.where(to < 288, to, to - 288)
    query = to - 576
    frame = jnp.where(to < 576, key // 9, query // OWN)
    row = jnp.where(to < 576, key % 9 + jnp.where(to < 288, 0, 9), query % OWN + 18)
    pick = (frame % NZ * NY + frame // NZ) * 24 + row
    move = (pick == lax.broadcasted_iota(jnp.int32, (count, count), 1)).astype(jnp.bfloat16)
    rows = jnp.dot(move, rows_ref[...], preferred_element_type=jnp.float32).astype(jnp.bfloat16)
    for i in range(NX):
        out_ref[i] = rows


def arrange(rows):
    return pl.pallas_call(
        arrange_kernel,
        in_specs=[VMEM],
        out_specs=VMEM,
        out_shape=jax.ShapeDtypeStruct((NX, NY * NZ * 24, COLS), jnp.bfloat16),
        compiler_params=pltpu.CompilerParams(vmem_limit_bytes=32 * 1024 * 1024),
        name="arrange",
    )(rows.reshape(NY * NZ * 24, COLS))


def finish_kernel(parts_ref, out_ref):
    shape = (NX, NZ, 8, HEAD_DIM)
    lane = lax.broadcasted_iota(jnp.int32, shape, 3)
    row = lax.broadcasted_iota(jnp.int32, shape, 2)
    for part in range(PARTS):
        words = parts_ref[:, part, :, OWN:OWN + 1, :128].astype(jnp.float32)
        for h in range(HEADS_HERE):
            cols = slice(h * HEAD_DIM, (h + 1) * HEAD_DIM)
            at = lane - (8 * row + 4 * h)
            top = jnp.sum(jnp.where((at == 0) | (at == 1), words, 0.0), axis=3, keepdims=True)
            total = jnp.sum(jnp.where((at == 2) | (at == 3), words, 0.0), axis=3, keepdims=True)
            top = jnp.where(total > 0, top, EMPTY)
            best = jnp.max(top, axis=(0, 1), keepdims=True)
            factor = jnp.where(total > 0, jnp.exp2(top - best), 0.0)
            whole = jnp.sum(total * factor, axis=(0, 1))
            numer = jnp.sum(parts_ref[:, part, :, :, cols].astype(jnp.float32) * factor, axis=(0, 1))
            result = (numer / whole).astype(jnp.bfloat16)
            start = part * COLS + h * HEAD_DIM
            out_ref[:, start:start + HEAD_DIM] = result[:OWN]


def finish(parts):
    return pl.pallas_call(
        finish_kernel,
        in_specs=[VMEM],
        out_specs=VMEM,
        out_shape=jax.ShapeDtypeStruct((OWN, PARTS * COLS), jnp.bfloat16),
        compiler_params=pltpu.CompilerParams(vmem_limit_bytes=48 * 1024 * 1024),
        name="finish",
    )(parts.reshape(NX, NY, NZ, 8, COLS))


def exchange(value, axis):
    return lax.all_to_all(value, axis, split_axis=0, concat_axis=0, tiled=True)


def spread(value, axis, count):
    return exchange(jnp.broadcast_to(value[None], (count,) + value.shape), axis)


def shards(
    encoded,
    block_source,
    block_slot,
    video_patches,
    latent_video,
    media_gain,
    queries,
    w_key,
    w_value,
):
    ax, az = lax.axis_index("x"), lax.axis_index("z")
    al, ac = lax.axis_index("yl"), lax.axis_index("c")
    head = al * 2 + ac
    slot = lax.dynamic_index_in_dim(block_slot[0], head, 0, keepdims=False)[:2]
    own = norm_slots(slot, encoded.reshape(NB, BLK, MEDIA), media_gain)
    slots = lax.all_gather(own, ("yh", "yl", "c"), axis=0, tiled=True)
    local = jnp.concatenate([w_key, w_value, queries], axis=0)
    local = jnp.transpose(local.reshape(24, PARTS, COLS), (1, 0, 2))
    note = jnp.pad(block_source.reshape(1, NB).astype(jnp.bfloat16), ((0, 7), (0, COLS - NB)))
    local = jnp.concatenate([local, jnp.broadcast_to(note[None], (PARTS, 8, COLS))], axis=1)
    column = exchange(local, "yh")
    cube = exchange(arrange(spread(column[:, :24], "z", NZ)), "x")

    source = column[:, 24, :NB].astype(jnp.int32).reshape(BLOCKS)
    block = jnp.arange(BLOCKS, dtype=jnp.int32)
    same = (source[:, None] == source[None, :]) & (block[None, :] < block[:, None])
    same = same & (block[:, None] // NB == block[None, :] // NB)
    rank = jnp.sum(same.astype(jnp.int32), axis=1)
    index = (block // NB * 4 + source) * 2 + rank
    ends = jnp.cumsum(video_patches)
    base = (ax * (NY * NZ) + az) * FRAME_ROWS
    info = jnp.concatenate([index, base[None].astype(jnp.int32), ends.astype(jnp.int32)]).astype(jnp.int32)

    which = (latent_video[:, None] == jnp.arange(VIDEOS)[None, :]).astype(jnp.int32)
    before = jnp.cumsum(which, axis=0) - which
    block_place = latent_video * NUM_LAT + LAT_BLK * jnp.sum(before * which, axis=1)
    place = (block_place[:, None] + jnp.arange(LAT_BLK)[None, :]).reshape(-1).astype(jnp.int32)

    target = jnp.pad(place.reshape(PADDED // 8, OWN), ((0, 0), (0, 8 - OWN)), constant_values=-1)
    message = attend(info, slots, cube, place, target)
    return finish(exchange(message.reshape(PADDED // 8, 8, COLS), ("x", "yh", "z")))


def solution(mesh):
    grid = Mesh(mesh.devices.reshape(NX, NY, NZ, 2, 2), ("x", "yh", "z", "yl", "c"))
    frame, head = ("x", "yh", "z"), ("yl", "c")
    placed = (
        P(frame + head, None),
        P(frame, None),
        P(frame, None, None),
        P(),
        P(),
        P(),
        P(frame, head),
        P(frame, head),
        P(frame, head),
    )
    return jax.shard_map(
        shards, mesh=grid, in_specs=placed, out_specs=P(frame, head), check_vma=False
    )
```
